32 devices in a mesh: chan: 8 (over z, y), tm: 4 (over x, core).
Axes of the slice: x: 2, y: 2, z: 4, core: 2. Of those that a mesh axis runs over, the one named last changes fastest.
Arguments:
- recording: bfloat16 [4096, 8192], P('chan', 'tm'), may hold values from -6 to 6
- band_taps: bfloat16 [3, 255], replicated, may hold values from -0.375 to 0.375
- channel_gain: float32 [4096], P('chan'), may hold values from 0.25 to 2
- range_test: bfloat16 [8192, 64], P('tm'), may hold values from -0.0625 to 0.0625
- corange_test: bfloat16 [64, 4096], P(None, 'chan'), may hold values from -0.09375 to 0.09375
- core_left: bfloat16 [128, 4096], P(None, 'chan'), may hold values from -0.09375 to 0.09375
- core_right: bfloat16 [8192, 128], P('tm'), may hold values from -0.0625 to 0.0625
Outputs:
- strain_rate: bfloat16 [3, 4096, 8192], P(None, 'chan', 'tm')
- range_sketch: float32 [3, 4096, 64], P(None, 'chan')
- corange_sketch: float32 [3, 64, 8192], P(None, None, 'tm')
- core_sketch: float32 [3, 128, 128], replicated
The draws below stay inside these ranges and needn't reach their ends.
All inputs are finite; a program needn't handle non-finite values.
Results may differ from the reference program's by a relative error of at most 0.0052.
Values may be sent and summed in bfloat16 or wider, within the bound.
A program may use at most 64 MiB of HBM per device.

```python
import math
import jax
import jax.numpy as jnp
from jax import lax

NBANDS = 3
TAPS = 255
RANGE = 64
CORANGE = 64
CORE = 128
HALF = 127
CHANNELS = 4096
SAMPLES = 8192


def shard_levels(key, shape, cuts, low, top_value):
    gain = 1.0
    for position, parts in cuts:
        heights = jax.random.uniform(jax.random.fold_in(jax.random.fold_in(key, 6), position), (parts,), jnp.float32, low / len(cuts), top_value / len(cuts))
        gain = gain * jnp.repeat(jnp.exp(heights), shape[position] // parts).reshape((-1,) + (1,) * (len(shape) - 1 - position))
    return gain


def normal_values(key, shape, deviation, limit, cuts=(), kind=jnp.bfloat16):
    level = shard_levels(key, shape, cuts, -0.22, 0.18) if cuts else 1.0
    result = jax.random.normal(key, shape, jnp.float32) * deviation * level
    return jnp.minimum(jnp.maximum(result, -limit), limit).astype(kind)


def setup_inputs(seed: int = 0) -> dict:
    splits = jax.random.split(jax.random.key(seed), 8)
    return {
        "recording": normal_values(splits[0], (CHANNELS, SAMPLES), 1.0, 6.0, ((0, 8), (1, 4))),
        "band_taps": normal_values(splits[1], (NBANDS, TAPS), TAPS ** -0.5, 0.375),
        "channel_gain": jnp.clip(jnp.exp(math.log(2.0) - 2.0794415 * jax.random.uniform(splits[2], (CHANNELS,), jnp.float32) ** shard_levels(splits[2], (CHANNELS,), ((0, 8),), -0.2, 0.2)), 0.25, 2.0),
        "range_test": normal_values(splits[3], (SAMPLES, RANGE), SAMPLES ** -0.5, 0.0625, ((0, 4),)),
        "corange_test": normal_values(splits[4], (CORANGE, CHANNELS), CHANNELS ** -0.5, 0.09375, ((1, 8),)),
        "core_left": normal_values(splits[5], (CORE, CHANNELS), CHANNELS ** -0.5, 0.09375, ((1, 8),)),
        "core_right": normal_values(splits[6], (SAMPLES, CORE), SAMPLES ** -0.5, 0.0625, ((0, 4),)),
    }


def reference(recording, band_taps, channel_gain, range_test, corange_test, core_left, core_right):
    length = SAMPLES + TAPS - 1
    signal_spec = jnp.fft.rfft(recording.astype(jnp.float32), n=length, axis=1)
    range_f = range_test.astype(jnp.float32)
    corange_f = corange_test.astype(jnp.float32)
    left_f = core_left.astype(jnp.float32)
    right_f = core_right.astype(jnp.float32)
    high = lax.Precision.HIGHEST

    def one_band(taps_row):
        flipped = taps_row.astype(jnp.float32)[::-1]
        spectrum = signal_spec * jnp.fft.rfft(flipped, n=length)
        full_conv = jnp.fft.irfft(spectrum, n=length, axis=1)
        filtered = full_conv[:, HALF:HALF + SAMPLES].astype(jnp.float32)
        filtered = filtered.astype(jnp.bfloat16).astype(jnp.float32)
        padded = jnp.pad(filtered, ((1, 1), (0, 0)))
        strain = (channel_gain[:, None] * (padded[2:] - padded[:-2])).astype(jnp.bfloat16)
        strain_f = strain.astype(jnp.float32)
        range_part = jnp.dot(strain_f, range_f, precision=high)
        corange_part = jnp.dot(corange_f, strain_f, precision=high)
        projected = jnp.dot(strain_f, right_f, precision=high)
        core_part = jnp.dot(left_f, projected, precision=high)
        return strain, range_part, corange_part, core_part

    strain_rate, range_sketch, corange_sketch, core_sketch = lax.map(one_band, band_taps)
    return strain_rate, range_sketch, corange_sketch, core_sketch
```

```python
import jax
import jax.numpy as jnp
from jax import lax
from jax.experimental import pallas as pl
from jax.experimental.pallas import tpu as pltpu
from jax.sharding import PartitionSpec as P

WIDE = 256
EDGE = 128
RIM = 16
F32 = jnp.float32
BF16 = jnp.bfloat16


def dot(a, b):
    return jnp.dot(a, b, preferred_element_type=F32)


def neighbours(low_part, high_part, axis):
    count = lax.axis_size(axis)
    forward = [(i, i + 1) for i in range(count - 1)]
    backward = [(target, source) for source, target in forward]
    return lax.ppermute(high_part, axis, forward), lax.ppermute(low_part, axis, backward)


def main_kernel(
    rec, left, right, low, high, vec, gain, rtest, ctest, weight, left_test,
    strain, rpart, core, ypart, toep_out,
    padded, toep, right_test, total,
):
    step = pl.program_id(0)
    rows, samples = rec.shape
    bands = vec.shape[0]
    own = pl.ds(RIM, rows)

    @pl.when(step == 0)
    def _():
        padded[own, EDGE : EDGE + samples] = rec[...]
        padded[own, 0:EDGE] = left[...]
        padded[own, EDGE + samples :] = right[...]
        padded[0:RIM, :] = low[...]
        padded[RIM + rows :, :] = high[...]
        for b in range(bands):
            spread = jnp.broadcast_to(vec[b : b + 1, :], (2 * WIDE, 2 * WIDE))
            skewed = pltpu.roll(spread, 0, 1, stride=1, stride_axis=0)
            toep[b] = skewed[:, :WIDE].astype(BF16)
        toep_out[...] = toep[...]
        right_test[:, 0:128] = ctest[...]
        right_test[:, 128:192] = rtest[...]
        right_test[:, 192:256] = jnp.zeros_like(rtest)
        both = dot(weight[...], padded[...])
        half = both.shape[0] // 2
        ypart[...] = both[:half] + both[half:]
        total[...] = jnp.zeros_like(total)

    start = pl.multiple_of(step * WIDE, WIDE)
    window = padded[:, pl.ds(start, 2 * WIDE)]
    test = right_test[pl.ds(start, WIDE), :]
    for b in range(bands):
        filtered = dot(window, toep[b]).astype(BF16).astype(F32)
        after = pltpu.roll(filtered, filtered.shape[0] - 1, 0)
        before = pltpu.roll(filtered, 1, 0)
        value = (gain[...] * (after - before)[RIM : RIM + rows]).astype(BF16)
        strain[b] = value
        total[b] += dot(value, test)

    @pl.when(step == pl.num_programs(0) - 1)
    def _():
        for b in range(bands):
            rpart[b] = total[b, :, 128:192]
            projected = total[b, :, 0:128]
            top = projected.astype(BF16)
            rest = (projected - top.astype(F32)).astype(BF16)
            core[b] = dot(left_test[...], top) + dot(left_test[...], rest)


def corange_kernel(ysum, toep, out):
    step = pl.program_id(0)
    start = pl.multiple_of(step * WIDE, WIDE)
    window = ysum[:, pl.ds(start, 2 * WIDE)].astype(BF16)
    for b in range(out.shape[0]):
        out[b] = dot(window, toep[b])


def whole(shape):
    return pl.BlockSpec(shape, lambda *_: (0,) * len(shape))


def on_device(recording, band_taps, channel_gain, range_test, corange_test, core_left, core_right):
    rows, samples = recording.shape
    bands, taps = band_taps.shape
    steps = samples // WIDE
    span = samples + 2 * EDGE
    left, right = neighbours(recording[:, :EDGE], recording[:, -EDGE:], "tm")
    first = jnp.concatenate([left[:1], recording[:1], right[:1]], axis=1)
    last = jnp.concatenate([left[-1:], recording[-1:], right[-1:]], axis=1)
    below, above = neighbours(first, last, "chan")
    low = jnp.pad(below, ((RIM - 1, 0), (0, 0)))
    high = jnp.pad(above, ((0, RIM - 1), (0, 0)))
    vec = jnp.pad(band_taps[:, ::-1].astype(F32), ((0, 0), (2 * WIDE - taps, 0)))
    scaled = corange_test.astype(F32) * channel_gain[None, :]
    weight = jnp.pad(scaled, ((0, 0), (RIM + 1, RIM - 1))) - jnp.pad(
        scaled, ((0, 0), (RIM - 1, RIM + 1))
    )
    top = weight.astype(BF16)
    rest = (weight - top.astype(F32)).astype(BF16)
    weight = jnp.concatenate([top, rest], axis=0)
    operands = (
        recording, left, right, low, high, vec, channel_gain[:, None],
        range_test, core_right, weight, core_left,
    )
    rank, core_rank, corank = range_test.shape[1], core_left.shape[0], corange_test.shape[0]
    strain, rpart, core, ypart, toep = pl.pallas_call(
        main_kernel,
        grid=(steps,),
        in_specs=[whole(x.shape) for x in operands],
        out_specs=[
            pl.BlockSpec((bands, rows, WIDE), lambda j: (0, 0, j)),
            whole((bands, rows, rank)),
            whole((bands, core_rank, core_rank)),
            whole((corank, span)),
            whole((bands, 2 * WIDE, WIDE)),
        ],
        out_shape=[
            jax.ShapeDtypeStruct((bands, rows, samples), BF16),
            jax.ShapeDtypeStruct((bands, rows, rank), F32),
            jax.ShapeDtypeStruct((bands, core_rank, core_rank), F32),
            jax.ShapeDtypeStruct((corank, span), F32),
            jax.ShapeDtypeStruct((bands, 2 * WIDE, WIDE), BF16),
        ],
        scratch_shapes=[
            pltpu.VMEM((rows + 2 * RIM, span), BF16),
            pltpu.VMEM((bands, 2 * WIDE, WIDE), BF16),
            pltpu.VMEM((samples, 256), BF16),
            pltpu.VMEM((bands, rows, 256), F32),
        ],
        compiler_params=pltpu.CompilerParams(vmem_limit_bytes=48 * 2**20),
    )(*operands)
    ysum = lax.psum(ypart, "chan")
    range_sketch = lax.psum(rpart, "tm")
    core_sketch = lax.psum(core, ("chan", "tm"))
    corange_sketch = pl.pallas_call(
        corange_kernel,
        grid=(steps,),
        in_specs=[whole(ysum.shape), whole(toep.shape)],
        out_specs=pl.BlockSpec((bands, corank, WIDE), lambda j: (0, 0, j)),
        out_shape=jax.ShapeDtypeStruct((bands, corank, samples), F32),
    )(ysum, toep)
    return strain, range_sketch, corange_sketch, core_sketch


def solution(mesh):
    in_specs = (
        P("chan", "tm"),
        P(),
        P("chan"),
        P("tm", None),
        P(None, "chan"),
        P(None, "chan"),
        P("tm", None),
    )
    out_specs = (P(None, "chan", "tm"), P(None, "chan", None), P(None, None, "tm"), P())
    return jax.shard_map(
        on_device, mesh=mesh, in_specs=in_specs, out_specs=out_specs, check_vma=False
    )
```

```python
import jax
import jax.numpy as jnp
from jax import lax
from jax.experimental import pallas as pl
from jax.experimental.pallas import tpu as pltpu
from jax.sharding import PartitionSpec as P

WIDE = 256
EDGE = 128
RIM = 16
F32 = jnp.float32
BF16 = jnp.bfloat16


def dot(a, b):
    return jnp.dot(a, b, preferred_element_type=F32)


def neighbours(low_part, high_part, axis):
    count = lax.axis_size(axis)
    forward = [(i, i + 1) for i in range(count - 1)]
    backward = [(target, source) for source, target in forward]
    return lax.ppermute(high_part, axis, forward), lax.ppermute(low_part, axis, backward)


def main_kernel(
    rec, left, right, low, high, vec, gain, rtest, ctest, weight, left_test,
    strain, rpart, core, ypart, toep_out,
    padded, toep, right_test, total,
):
    step = pl.program_id(0)
    rows, samples = rec.shape
    bands = vec.shape[0]
    own = pl.ds(RIM, rows)

    @pl.when(step == 0)
    def _():
        padded[own, EDGE : EDGE + samples] = rec[...]
        padded[own, 0:EDGE] = left[...]
        padded[own, EDGE + samples :] = right[...]
        padded[0:RIM, :] = low[...]
        padded[RIM + rows :, :] = high[...]
        for b in range(bands):
            spread = jnp.broadcast_to(vec[b : b + 1, :], (2 * WIDE, 2 * WIDE))
            skewed = pltpu.roll(spread, 0, 1, stride=1, stride_axis=0)
            toep[b] = skewed[:, :WIDE].astype(BF16)
        toep_out[...] = toep[...]
        right_test[:, 0:128] = ctest[...]
        right_test[:, 128:192] = rtest[...]
        right_test[:, 192:256] = jnp.zeros_like(rtest)
        both = dot(weight[...], padded[...])
        half = both.shape[0] // 2
        ypart[...] = both[:half] + both[half:]
        total[...] = jnp.zeros_like(total)

    start = pl.multiple_of(step * WIDE, WIDE)
    window = padded[:, pl.ds(start, 2 * WIDE)]
    test = right_test[pl.ds(start, WIDE), :]
    for b in range(bands):
        filtered = dot(window, toep[b]).astype(BF16).astype(F32)
        after = pltpu.roll(filtered, filtered.shape[0] - 1, 0)
        before = pltpu.roll(filtered, 1, 0)
        value = (gain[...] * (after - before)[RIM : RIM + rows]).astype(BF16)
        strain[b] = value
        total[b] += dot(value, test)

    @pl.when(step == pl.num_programs(0) - 1)
    def _():
        for b in range(bands):
            for c in range(rows // 128):
                turned = total[b, c * 128 : (c + 1) * 128, 128:256].T
                at = (c * bands + b) * rtest.shape[1]
                rpart[at : at + rtest.shape[1], :] = turned[: rtest.shape[1]]
            projected = total[b, :, 0:128]
            top = projected.astype(BF16)
            rest = (projected - top.astype(F32)).astype(BF16)
            core[b * 128 : (b + 1) * 128, :] = dot(left_test[...], top) + dot(left_test[...], rest)


def share_kernel(
    rpart, core, ypart, toep, rout, yout, cout,
    tm_send, tm_recv, rall, csend, call, y_send, y_recv, yall, yfull,
    tm_sems, r_sems, c_sems, call_sems, y_sems, yall_sems,
):
    times, blocks = rall.shape[0], yall.shape[0]
    here_t, here_c = lax.axis_index("tm"), lax.axis_index("chan")
    bands, rank, rows = rout.shape
    nr, nc = rall.shape[1], call.shape[1]
    span = ypart.shape[1]
    piece, width = ypart.shape[0] // blocks, yall.shape[2]

    def peer(axis, d):
        if axis == "tm":
            return lax.rem(here_t + d, times)
        return lax.rem(here_c + d, blocks)

    def send(src, dst, sems, axis, d):
        copy = pltpu.make_async_remote_copy(
            src_ref=src, dst_ref=dst, send_sem=sems.at[0, d - 1], recv_sem=sems.at[1, d - 1],
            device_id={axis: peer(axis, d)}, device_id_type=pl.DeviceIdType.MESH,
        )
        copy.start()
        return copy

    barrier = pltpu.get_barrier_semaphore()
    for axis, count in (("tm", times), ("chan", blocks)):
        for d in range(1, count):
            pl.semaphore_signal(
                barrier, inc=1, device_id={axis: peer(axis, d)},
                device_id_type=pl.DeviceIdType.MESH,
            )
    for p in range(blocks):
        block = ypart[p * piece : (p + 1) * piece, :]
        if width < span:
            block = jnp.concatenate(
                [block[:, k : k + width] for k in range(0, span, width)], axis=0
            )
        elif piece < RIM:
            block = jnp.concatenate([block, jnp.zeros((RIM - piece, span), F32)], axis=0)
        y_send[p] = block.astype(BF16)
    for q in range(times):
        tm_send[q, 0:nr] = rpart[q * nr : (q + 1) * nr, :].astype(BF16)
        tm_send[q, nr : nr + nc] = core[q * nc : (q + 1) * nc, :].astype(BF16)
    pl.semaphore_wait(barrier, times + blocks - 2)

    tm_copies = [
        send(tm_send.at[peer("tm", d)], tm_recv.at[d - 1], tm_sems, "tm", d)
        for d in range(1, times)
    ]
    y_copies = [
        send(y_send.at[peer("chan", d)], y_recv.at[d - 1], y_sems, "chan", d)
        for d in range(1, blocks)
    ]
    summed = tm_send[here_t].astype(F32)
    for d in range(1, times):
        tm_copies[d - 1].wait_recv()
        summed += tm_recv[d - 1].astype(F32)
    rall[here_t] = summed[0:nr].astype(BF16)
    call[here_c] = summed[nr : nr + nc].astype(BF16)
    c_copies = [
        send(call.at[here_c], call.at[here_c], call_sems, "chan", d) for d in range(1, blocks)
    ]
    r_copies = [send(rall.at[here_t], rall.at[here_t], r_sems, "tm", d) for d in range(1, times)]

    y_sum = y_send[here_c].astype(F32)
    for d in range(1, blocks):
        y_copies[d - 1].wait_recv()
        y_sum += y_recv[d - 1].astype(F32)
    yall[here_c] = y_sum.astype(BF16)
    yall_copies = [
        send(yall.at[here_c], yall.at[here_c], yall_sems, "chan", d) for d in range(1, blocks)
    ]

    for copy in c_copies:
        copy.wait_recv()
    c_sum = call[0].astype(F32)
    for p in range(1, blocks):
        c_sum += call[p].astype(F32)
    csend[here_t] = c_sum
    core_copies = [
        send(csend.at[here_t], csend.at[here_t], c_sems, "tm", d) for d in range(1, times)
    ]

    for copy in r_copies:
        copy.wait_recv()
    per = nr // RIM
    for c in range(rows // 128):
        for b in range(bands):
            for k in range(rank // RIM):
                at = ((c * bands + b) * rank) // RIM + k
                part = rall[at // per, (at % per) * RIM : (at % per + 1) * RIM, :]
                rout[b, k * RIM : (k + 1) * RIM, c * 128 : (c + 1) * 128] = part.astype(F32)

    for copy in yall_copies:
        copy.wait_recv()
    for p in range(blocks):
        block = yall[p].astype(F32)[: piece * (span // width)]
        if width < span:
            block = jnp.concatenate(
                [block[k * piece : (k + 1) * piece] for k in range(span // width)], axis=1
            )
        yfull[p * piece : (p + 1) * piece, :] = block
    corank, samples = yout.shape[1:]
    window = jnp.concatenate(
        [yfull[:, k : k + 2 * WIDE].astype(BF16) for k in range(0, samples, WIDE)], axis=0
    )
    for b in range(bands):
        result = dot(window, toep[b])
        for k in range(samples // WIDE):
            yout[b, :, k * WIDE : (k + 1) * WIDE] = result[k * corank : (k + 1) * corank]

    for copy in core_copies:
        copy.wait_recv()
    for q in range(times):
        cout[q * nc : (q + 1) * nc, :] = csend[q]
    for copy in tm_copies + y_copies + c_copies + r_copies + yall_copies + core_copies:
        copy.wait_send()


def whole(shape):
    return pl.BlockSpec(shape, lambda *_: (0,) * len(shape))


def on_device(recording, band_taps, channel_gain, range_test, corange_test, core_left, core_right):
    rows, samples = recording.shape
    bands, taps = band_taps.shape
    steps = samples // WIDE
    span = samples + 2 * EDGE
    left, right = neighbours(recording[:, :EDGE], recording[:, -EDGE:], "tm")
    first = jnp.concatenate([left[:1], recording[:1], right[:1]], axis=1)
    last = jnp.concatenate([left[-1:], recording[-1:], right[-1:]], axis=1)
    below, above = neighbours(first, last, "chan")
    low = jnp.pad(below, ((RIM - 1, 0), (0, 0)))
    high = jnp.pad(above, ((0, RIM - 1), (0, 0)))
    vec = jnp.pad(band_taps[:, ::-1].astype(F32), ((0, 0), (2 * WIDE - taps, 0)))
    scaled = corange_test.astype(F32) * channel_gain[None, :]
    weight = jnp.pad(scaled, ((0, 0), (RIM + 1, RIM - 1))) - jnp.pad(
        scaled, ((0, 0), (RIM - 1, RIM + 1))
    )
    top = weight.astype(BF16)
    rest = (weight - top.astype(F32)).astype(BF16)
    weight = jnp.concatenate([top, rest], axis=0)
    operands = (
        recording, left, right, low, high, vec, channel_gain[:, None],
        range_test, core_right, weight, core_left,
    )
    rank, core_rank, corank = range_test.shape[1], core_left.shape[0], corange_test.shape[0]
    strain, rpart, core, ypart, toep = pl.pallas_call(
        main_kernel,
        grid=(steps,),
        in_specs=[whole(x.shape) for x in operands],
        out_specs=[
            pl.BlockSpec((bands, rows, WIDE), lambda j: (0, 0, j)),
            whole((bands * rank * rows // 128, 128)),
            whole((bands * core_rank, core_rank)),
            whole((corank, span)),
            whole((bands, 2 * WIDE, WIDE)),
        ],
        out_shape=[
            jax.ShapeDtypeStruct((bands, rows, samples), BF16),
            jax.ShapeDtypeStruct((bands * rank * rows // 128, 128), F32),
            jax.ShapeDtypeStruct((bands * core_rank, core_rank), F32),
            jax.ShapeDtypeStruct((corank, span), F32),
            jax.ShapeDtypeStruct((bands, 2 * WIDE, WIDE), BF16),
        ],
        scratch_shapes=[
            pltpu.VMEM((rows + 2 * RIM, span), BF16),
            pltpu.VMEM((bands, 2 * WIDE, WIDE), BF16),
            pltpu.VMEM((samples, 256), BF16),
            pltpu.VMEM((bands, rows, 256), F32),
        ],
        compiler_params=pltpu.CompilerParams(vmem_limit_bytes=48 * 2**20),
    )(*operands)
    times, blocks = lax.axis_size("tm"), lax.axis_size("chan")
    nr, nc = rpart.shape[0] // times, core.shape[0] // times
    piece = corank // blocks
    fold = max(1, RIM // piece)
    if span % (fold * 128):
        fold = 1
    tile = (max(RIM, piece), span // fold)
    vmem = pl.BlockSpec(memory_space=pltpu.VMEM)

    def sems(count):
        return pltpu.SemaphoreType.DMA((2, count - 1))

    ranges, corange_sketch, core_sketch = pl.pallas_call(
        share_kernel,
        in_specs=[vmem] * 4,
        out_specs=[vmem] * 3,
        out_shape=[
            jax.ShapeDtypeStruct((bands, rank, rows), F32),
            jax.ShapeDtypeStruct((bands, corank, samples), F32),
            jax.ShapeDtypeStruct((bands * core_rank, core_rank), F32),
        ],
        scratch_shapes=[
            pltpu.VMEM((times, nr + nc, 128), BF16),
            pltpu.VMEM((times - 1, nr + nc, 128), BF16),
            pltpu.VMEM((times, nr, 128), BF16),
            pltpu.VMEM((times, nc, 128), F32),
            pltpu.VMEM((blocks, nc, 128), BF16),
            pltpu.VMEM((blocks,) + tile, BF16),
            pltpu.VMEM((blocks - 1,) + tile, BF16),
            pltpu.VMEM((blocks,) + tile, BF16),
            pltpu.VMEM((corank, span), F32),
            sems(times), sems(times), sems(times), sems(blocks), sems(blocks), sems(blocks),
        ],
        compiler_params=pltpu.CompilerParams(
            collective_id=0, has_side_effects=True, vmem_limit_bytes=40 * 2**20
        ),
    )(rpart, core, ypart, toep)
    range_sketch = jnp.swapaxes(ranges, 1, 2)
    core_sketch = core_sketch.reshape(bands, core_rank, core_rank)
    return strain, range_sketch, corange_sketch, core_sketch


def solution(mesh):
    in_specs = (
        P("chan", "tm"),
        P(),
        P("chan"),
        P("tm", None),
        P(None, "chan"),
        P(None, "chan"),
        P("tm", None),
    )
    out_specs = (P(None, "chan", "tm"), P(None, "chan", None), P(None, None, "tm"), P())
    return jax.shard_map(
        on_device, mesh=mesh, in_specs=in_specs, out_specs=out_specs, check_vma=False
    )
```

```python
import jax
import jax.numpy as jnp
from jax import lax
from jax.experimental import pallas as pl
from jax.experimental.pallas import tpu as pltpu
from jax.sharding import PartitionSpec as P

WIDE = 256
EDGE = 128
RIM = 16
F32 = jnp.float32
BF16 = jnp.bfloat16


def dot(a, b):
    return jnp.dot(a, b, preferred_element_type=F32)


def fused_kernel(
    rec, taps, gain, rtest, ctest, corange, left_test,
    strain, rout, yout, cout,
    padded, toep, right_test, gains, total,
    tm_send, tm_recv, rall, csend, call, y_send, y_recv, yall, yfull,
    tm_sems, r_sems, c_sems, call_sems, y_sems, yall_sems, halo_sems, own_sem,
):
    times, blocks = rall.shape[0], yall.shape[0]
    here_t, here_c = lax.axis_index("tm"), lax.axis_index("chan")
    bands, rank, rows = rout.shape
    samples = rec.shape[1]
    nr, nc = rall.shape[1], call.shape[1]
    span = padded.shape[1]
    corank = corange.shape[0]
    piece, width = corank // blocks, yall.shape[2]
    steps = samples // WIDE
    tail = EDGE + samples

    def peer(axis, d):
        if axis == "tm":
            return lax.rem(here_t + d, times)
        return lax.rem(here_c + d, blocks)

    def send(src, dst, sems, axis, d):
        copy = pltpu.make_async_remote_copy(
            src_ref=src, dst_ref=dst, send_sem=sems.at[0, d - 1], recv_sem=sems.at[1, d - 1],
            device_id={axis: peer(axis, d)}, device_id_type=pl.DeviceIdType.MESH,
        )
        copy.start()
        return copy

    around = [(c, t) for c in (-1, 0, 1) for t in (-1, 0, 1) if (c, t) != (0, 0)]

    def place(c, t):
        return {"chan": peer("chan", c + blocks), "tm": peer("tm", t + times)}

    barrier = pltpu.get_barrier_semaphore()
    for axis, count in (("tm", times), ("chan", blocks)):
        for d in range(1, count):
            pl.semaphore_signal(
                barrier, inc=1, device_id={axis: peer(axis, d)},
                device_id_type=pl.DeviceIdType.MESH,
            )
    for c, t in around:
        if c and t:
            pl.semaphore_signal(
                barrier, inc=1, device_id=place(c, t), device_id_type=pl.DeviceIdType.MESH
            )
    own = pltpu.make_async_copy(
        rec, padded.at[RIM : RIM + rows, EDGE : EDGE + samples], own_sem
    )
    own.start()
    pl.semaphore_wait(barrier, times + blocks - 2 + 4)
    row_from = {-1: slice(0, RIM), 0: slice(0, rows), 1: slice(rows - RIM, rows)}
    row_to = {-1: slice(RIM + rows, None), 0: slice(RIM, RIM + rows), 1: slice(0, RIM)}
    col_from = {-1: slice(0, EDGE), 0: slice(0, samples), 1: slice(samples - EDGE, samples)}
    col_to = {-1: slice(tail, span), 0: slice(EDGE, tail), 1: slice(0, EDGE)}
    row_to[-1] = slice(RIM + rows, rows + 2 * RIM)
    halos = []
    for i, (c, t) in enumerate(around):
        copy = pltpu.make_async_remote_copy(
            src_ref=rec.at[row_from[c], col_from[t]],
            dst_ref=padded.at[row_to[c], col_to[t]],
            send_sem=halo_sems.at[0, i], recv_sem=halo_sems.at[1, i],
            device_id=place(c, t), device_id_type=pl.DeviceIdType.MESH,
        )
        copy.start()
        halos.append(copy)

    for b in range(bands):
        spread = jnp.broadcast_to(taps[b : b + 1, :], (WIDE, 2 * WIDE))
        skewed = pltpu.roll(spread, 1, 1, stride=1, stride_axis=0)
        toep[b] = skewed.T.astype(BF16)
    right_test[:, 0:128] = ctest[...]
    turned = jnp.concatenate([rtest[...].astype(F32), jnp.zeros(rtest.shape, F32)], axis=0)
    right_test[:, 128:256] = turned.T.astype(BF16)
    column = jnp.broadcast_to(gain[...], (128, rows)).T
    gains[...] = jnp.concatenate([column, column], axis=1)
    total[...] = jnp.zeros_like(total)
    scaled = corange[...].astype(F32) * gain[...]
    lane = lax.broadcasted_iota(jnp.int32, scaled.shape, 1)
    weight = jnp.where(lane == 0, 0.0, pltpu.roll(scaled, 1, 1)) - jnp.where(
        lane == rows - 1, 0.0, pltpu.roll(scaled, rows - 1, 1)
    )
    top = weight.astype(BF16)
    rest = (weight - top.astype(F32)).astype(BF16)
    weight = jnp.concatenate([top, rest], axis=0)
    own.wait()
    for copy in halos:
        copy.wait()

    @pl.when(here_t == 0)
    def _():
        padded[:, 0:EDGE] = jnp.zeros((rows + 2 * RIM, EDGE), BF16)

    @pl.when(here_t == times - 1)
    def _():
        padded[:, tail:span] = jnp.zeros((rows + 2 * RIM, EDGE), BF16)

    @pl.when(here_c == 0)
    def _():
        padded[0:RIM, :] = jnp.zeros((RIM, span), BF16)

    @pl.when(here_c == blocks - 1)
    def _():
        padded[RIM + rows : rows + 2 * RIM, :] = jnp.zeros((RIM, span), BF16)

    both = dot(weight, padded[RIM : RIM + rows, :])
    before_row = padded[0:RIM, :].astype(F32)[RIM - 1 : RIM]
    after_row = padded[RIM + rows : rows + 2 * RIM, :].astype(F32)[0:1]
    yfull[...] = (
        both[:corank] + both[corank:]
        + scaled[:, rows - 1 : rows] * after_row - scaled[:, 0:1] * before_row
    )
    for p in range(blocks):
        block = yfull[p * piece : (p + 1) * piece, :]
        if width < span:
            block = jnp.concatenate(
                [block[:, k : k + width] for k in range(0, span, width)], axis=0
            )
        elif piece < RIM:
            block = jnp.concatenate([block, jnp.zeros((RIM - piece, span), F32)], axis=0)
        y_send[p] = block.astype(BF16)
    y_copies = [
        send(y_send.at[peer("chan", d)], y_recv.at[d - 1], y_sems, "chan", d)
        for d in range(1, blocks)
    ]

    def filter_step(step, carry):
        start = pl.multiple_of(step * WIDE, WIDE)
        window = padded[:, pl.ds(start, 2 * WIDE)]
        test = right_test[pl.ds(start, WIDE), :]
        for b in range(bands):
            filtered = dot(window, toep[b]).astype(BF16).astype(F32)
            after = pltpu.roll(filtered, filtered.shape[0] - 1, 0)
            before = pltpu.roll(filtered, 1, 0)
            value = (gains[...] * (after - before)[RIM : RIM + rows]).astype(BF16)
            strain[b, :, pl.ds(start, WIDE)] = value
            total[b] += dot(value, test)
        return carry

    half = (3 * steps) // 4
    lax.fori_loop(0, half, filter_step, 0)
    y_sum = y_send[here_c].astype(F32)
    for d in range(1, blocks):
        y_copies[d - 1].wait_recv()
        y_sum += y_recv[d - 1].astype(F32)
    yall[here_c] = y_sum.astype(BF16)
    yall_copies = [
        send(yall.at[here_c], yall.at[here_c], yall_sems, "chan", d) for d in range(1, blocks)
    ]

    lax.fori_loop(half, steps, filter_step, 0)

    for c in range(rows // 128):
        for b in range(bands):
            part = total[b, c * 128 : (c + 1) * 128, 128:256].T[:rank].astype(BF16)
            for k in range(rank // RIM):
                at = (c * bands + b) * rank + k * RIM
                row = at % nr
                tm_send[at // nr, row : row + RIM] = part[k * RIM : (k + 1) * RIM]
    order = left_test.shape[0]
    for b in range(bands):
        projected = total[b, :, 0:128]
        top = projected.astype(BF16)
        rest = (projected - top.astype(F32)).astype(BF16)
        term = (dot(left_test[...], top) + dot(left_test[...], rest)).astype(BF16)
        for k in range(order // RIM):
            at = b * order + k * RIM
            row = nr + at % nc
            tm_send[at // nc, row : row + RIM] = term[k * RIM : (k + 1) * RIM]
    tm_copies = [
        send(tm_send.at[peer("tm", d)], tm_recv.at[d - 1], tm_sems, "tm", d)
        for d in range(1, times)
    ]
    summed = tm_send[here_t].astype(F32)
    for d in range(1, times):
        tm_copies[d - 1].wait_recv()
        summed += tm_recv[d - 1].astype(F32)
    rall[here_t] = summed[0:nr].astype(BF16)
    call[here_c] = summed[nr : nr + nc].astype(BF16)
    c_copies = [
        send(call.at[here_c], call.at[here_c], call_sems, "chan", d) for d in range(1, blocks)
    ]
    r_copies = [send(rall.at[here_t], rall.at[here_t], r_sems, "tm", d) for d in range(1, times)]

    for copy in yall_copies:
        copy.wait_recv()
    for p in range(blocks):
        block = yall[p].astype(F32)[: piece * (span // width)]
        if width < span:
            block = jnp.concatenate(
                [block[k * piece : (k + 1) * piece] for k in range(span // width)], axis=1
            )
        yfull[p * piece : (p + 1) * piece, :] = block
    window = jnp.concatenate(
        [yfull[:, k : k + 2 * WIDE].astype(BF16) for k in range(0, samples, WIDE)], axis=0
    )
    for b in range(bands):
        result = dot(window, toep[b])
        for k in range(samples // WIDE):
            yout[b, :, k * WIDE : (k + 1) * WIDE] = result[k * corank : (k + 1) * corank]

    for copy in c_copies:
        copy.wait_recv()
    c_sum = call[0].astype(F32)
    for p in range(1, blocks):
        c_sum += call[p].astype(F32)
    csend[here_t] = c_sum
    core_copies = [
        send(csend.at[here_t], csend.at[here_t], c_sems, "tm", d) for d in range(1, times)
    ]

    for copy in r_copies:
        copy.wait_recv()
    per = nr // RIM
    for c in range(rows // 128):
        for b in range(bands):
            for k in range(rank // RIM):
                at = ((c * bands + b) * rank) // RIM + k
                part = rall[at // per, (at % per) * RIM : (at % per + 1) * RIM, :]
                rout[b, k * RIM : (k + 1) * RIM, c * 128 : (c + 1) * 128] = part.astype(F32)

    for copy in core_copies:
        copy.wait_recv()
    for q in range(times):
        cout[q * nc : (q + 1) * nc, :] = csend[q]
    for copy in tm_copies + y_copies + c_copies + r_copies + yall_copies + core_copies:
        copy.wait_send()


def on_device(recording, band_taps, channel_gain, range_test, corange_test, core_left, core_right):
    rows, samples = recording.shape
    bands, taps = band_taps.shape
    span = samples + 2 * EDGE
    rank, core_rank, corank = range_test.shape[1], core_left.shape[0], corange_test.shape[0]
    times, blocks = lax.axis_size("tm"), lax.axis_size("chan")
    nr, nc = bands * rank * rows // 128 // times, bands * core_rank // times
    piece = corank // blocks
    fold = max(1, RIM // piece)
    if span % (fold * 128):
        fold = 1
    tile = (max(RIM, piece), span // fold)
    vmem = pl.BlockSpec(memory_space=pltpu.VMEM)
    anywhere = pl.BlockSpec(memory_space=pl.ANY)

    def sems(count):
        return pltpu.SemaphoreType.DMA((2, count - 1))

    strain, ranges, corange_sketch, core_sketch = pl.pallas_call(
        fused_kernel,
        in_specs=[anywhere] + [vmem] * 6,
        out_specs=[vmem] * 4,
        out_shape=[
            jax.ShapeDtypeStruct((bands, rows, samples), BF16),
            jax.ShapeDtypeStruct((bands, rank, rows), F32),
            jax.ShapeDtypeStruct((bands, corank, samples), F32),
            jax.ShapeDtypeStruct((bands * core_rank, core_rank), F32),
        ],
        scratch_shapes=[
            pltpu.VMEM((rows + 2 * RIM, span), BF16),
            pltpu.VMEM((bands, 2 * WIDE, WIDE), BF16),
            pltpu.VMEM((samples, 256), BF16),
            pltpu.VMEM((rows, WIDE), F32),
            pltpu.VMEM((bands, rows, 256), F32),
            pltpu.VMEM((times, nr + nc, 128), BF16),
            pltpu.VMEM((times - 1, nr + nc, 128), BF16),
            pltpu.VMEM((times, nr, 128), BF16),
            pltpu.VMEM((times, nc, 128), F32),
            pltpu.VMEM((blocks, nc, 128), BF16),
            pltpu.VMEM((blocks,) + tile, BF16),
            pltpu.VMEM((blocks - 1,) + tile, BF16),
            pltpu.VMEM((blocks,) + tile, BF16),
            pltpu.VMEM((corank, span), F32),
            sems(times), sems(times), sems(times), sems(blocks), sems(blocks), sems(blocks),
            sems(9),
            pltpu.SemaphoreType.DMA,
        ],
        compiler_params=pltpu.CompilerParams(
            collective_id=0, has_side_effects=True, vmem_limit_bytes=36 * 2**20
        ),
    )(
        recording,
        jnp.pad(band_taps.astype(F32), ((0, 0), (0, 2 * WIDE - taps))),
        channel_gain[None, :],
        range_test.T,
        core_right,
        corange_test,
        core_left,
    )
    range_sketch = jnp.swapaxes(ranges, 1, 2)
    core_sketch = core_sketch.reshape(bands, core_rank, core_rank)
    return strain, range_sketch, corange_sketch, core_sketch


def solution(mesh):
    in_specs = (
        P("chan", "tm"),
        P(),
        P("chan"),
        P("tm", None),
        P(None, "chan"),
        P(None, "chan"),
        P("tm", None),
    )
    out_specs = (P(None, "chan", "tm"), P(None, "chan", None), P(None, None, "tm"), P())
    return jax.shard_map(
        on_device, mesh=mesh, in_specs=in_specs, out_specs=out_specs, check_vma=False
    )
```

```python
import jax
import jax.numpy as jnp
from jax import lax
from jax.experimental import pallas as pl
from jax.experimental.pallas import tpu as pltpu
from jax.sharding import PartitionSpec as P

WIDE = 256
EDGE = 128
RIM = 16
F32 = jnp.float32
BF16 = jnp.bfloat16


def dot(a, b):
    return jnp.dot(a, b, preferred_element_type=F32)


def fused_kernel(
    rec, taps, gain, rtest_hbm, ctest_hbm, corange_hbm, left_hbm,
    strain, rout, yout, cout,
    padded, toep, right_test, gains, total, stage, out_sems,
    tm_send, tm_recv, rall, csend, call, y_send, y_recv, yall, yfull,
    tm_sems, r_sems, c_sems, call_sems, y_sems, yall_sems, halo_sems, own_sem,
    rtest, ctest, corange, left_test, in_sems,
):
    times, blocks = rall.shape[1], yall.shape[0]
    here_t, here_c = lax.axis_index("tm"), lax.axis_index("chan")
    bands, rank, rows = rout.shape
    samples = rec.shape[1]
    nr, nc = rall.shape[2], call.shape[2]
    span = padded.shape[1]
    corank = corange.shape[0]
    piece, width = corank // blocks, yall.shape[2]
    steps = samples // WIDE
    tail = EDGE + samples

    def peer(axis, d):
        if axis == "tm":
            return lax.rem(here_t + d, times)
        return lax.rem(here_c + d, blocks)

    def send(src, dst, sems, axis, d, b=0):
        at = b * ((times if axis == "tm" else blocks) - 1) + d - 1
        copy = pltpu.make_async_remote_copy(
            src_ref=src, dst_ref=dst, send_sem=sems.at[0, at], recv_sem=sems.at[1, at],
            device_id={axis: peer(axis, d)}, device_id_type=pl.DeviceIdType.MESH,
        )
        copy.start()
        return copy

    around = [(c, t) for c in (-1, 0, 1) for t in (-1, 0, 1) if (c, t) != (0, 0)]

    def place(c, t):
        return {"chan": peer("chan", c + blocks), "tm": peer("tm", t + times)}

    barrier = pltpu.get_barrier_semaphore()
    for axis, count in (("tm", times), ("chan", blocks)):
        for d in range(1, count):
            pl.semaphore_signal(
                barrier, inc=1, device_id={axis: peer(axis, d)},
                device_id_type=pl.DeviceIdType.MESH,
            )
    for c, t in around:
        if c and t:
            pl.semaphore_signal(
                barrier, inc=1, device_id=place(c, t), device_id_type=pl.DeviceIdType.MESH
            )
    own = pltpu.make_async_copy(
        rec, padded.at[RIM : RIM + rows, EDGE : EDGE + samples], own_sem
    )
    own.start()
    inputs = []
    for i, (src, dst) in enumerate(
        ((rtest_hbm, rtest), (ctest_hbm, ctest), (corange_hbm, corange), (left_hbm, left_test))
    ):
        inputs.append(pltpu.make_async_copy(src, dst, in_sems.at[i]))
        inputs[-1].start()
    pl.semaphore_wait(barrier, times + blocks - 2 + 4)
    row_from = {-1: slice(0, RIM), 0: slice(0, rows), 1: slice(rows - RIM, rows)}
    row_to = {-1: slice(RIM + rows, None), 0: slice(RIM, RIM + rows), 1: slice(0, RIM)}
    col_from = {-1: slice(0, EDGE), 0: slice(0, samples), 1: slice(samples - EDGE, samples)}
    col_to = {-1: slice(tail, span), 0: slice(EDGE, tail), 1: slice(0, EDGE)}
    row_to[-1] = slice(RIM + rows, rows + 2 * RIM)
    halos = []
    for i, (c, t) in enumerate(around):
        copy = pltpu.make_async_remote_copy(
            src_ref=rec.at[row_from[c], col_from[t]],
            dst_ref=padded.at[row_to[c], col_to[t]],
            send_sem=halo_sems.at[0, i], recv_sem=halo_sems.at[1, i],
            device_id=place(c, t), device_id_type=pl.DeviceIdType.MESH,
        )
        copy.start()
        halos.append(copy)

    for b in range(bands):
        spread = jnp.broadcast_to(taps[b : b + 1, :], (WIDE, 2 * WIDE))
        skewed = pltpu.roll(spread, 1, 1, stride=1, stride_axis=0)
        toep[b] = skewed.T.astype(BF16)
    for copy in inputs:
        copy.wait()
    right_test[:, 0:128] = ctest[...]
    turned = jnp.concatenate([rtest[...].astype(F32), jnp.zeros(rtest.shape, F32)], axis=0)
    right_test[:, 128:256] = turned.T.astype(BF16)
    column = jnp.broadcast_to(gain[...], (128, rows)).T
    gains[...] = jnp.concatenate([column, column], axis=1)
    total[...] = jnp.zeros_like(total)
    scaled = corange[...].astype(F32) * gain[...]
    lane = lax.broadcasted_iota(jnp.int32, scaled.shape, 1)
    weight = jnp.where(lane == 0, 0.0, pltpu.roll(scaled, 1, 1)) - jnp.where(
        lane == rows - 1, 0.0, pltpu.roll(scaled, rows - 1, 1)
    )
    top = weight.astype(BF16)
    rest = (weight - top.astype(F32)).astype(BF16)
    weight = jnp.concatenate([top, rest], axis=0)
    own.wait()
    for copy in halos:
        copy.wait()

    @pl.when(here_t == 0)
    def _():
        padded[:, 0:EDGE] = jnp.zeros((rows + 2 * RIM, EDGE), BF16)

    @pl.when(here_t == times - 1)
    def _():
        padded[:, tail:span] = jnp.zeros((rows + 2 * RIM, EDGE), BF16)

    @pl.when(here_c == 0)
    def _():
        padded[0:RIM, :] = jnp.zeros((RIM, span), BF16)

    @pl.when(here_c == blocks - 1)
    def _():
        padded[RIM + rows : rows + 2 * RIM, :] = jnp.zeros((RIM, span), BF16)

    both = dot(weight, padded[RIM : RIM + rows, :])
    before_row = padded[0:RIM, :].astype(F32)[RIM - 1 : RIM]
    after_row = padded[RIM + rows : rows + 2 * RIM, :].astype(F32)[0:1]
    yfull[...] = (
        both[:corank] + both[corank:]
        + scaled[:, rows - 1 : rows] * after_row - scaled[:, 0:1] * before_row
    )
    for p in range(blocks):
        block = yfull[p * piece : (p + 1) * piece, :]
        if width < span:
            block = jnp.concatenate(
                [block[:, k : k + width] for k in range(0, span, width)], axis=0
            )
        elif piece < RIM:
            block = jnp.concatenate([block, jnp.zeros((RIM - piece, span), F32)], axis=0)
        y_send[p] = block.astype(BF16)
    y_copies = [
        send(y_send.at[peer("chan", d)], y_recv.at[d - 1], y_sems, "chan", d)
        for d in range(1, blocks)
    ]

    out_copies = []

    def filter_band(b):
        def filter_step(step, carry):
            start = pl.multiple_of(step * WIDE, WIDE)
            window = padded[:, pl.ds(start, 2 * WIDE)]
            filtered = dot(window, toep[b]).astype(BF16).astype(F32)
            after = pltpu.roll(filtered, filtered.shape[0] - 1, 0)
            before = pltpu.roll(filtered, 1, 0)
            value = (gains[...] * (after - before)[RIM : RIM + rows]).astype(BF16)
            stage[b, :, pl.ds(start, WIDE)] = value
            total[b] += dot(value, right_test[pl.ds(start, WIDE), :])
            return carry

        lax.fori_loop(0, steps, filter_step, 0)
        out_copies.append(pltpu.make_async_copy(stage.at[b], strain.at[b], out_sems.at[b]))
        out_copies[-1].start()

    started = []

    def spread_terms(b):
        for c in range(rows // 128):
            part = total[b, c * 128 : (c + 1) * 128, 128:256].T[:rank].astype(BF16)
            for k in range(rank // RIM):
                at = c * rank + k * RIM
                row = at % nr
                tm_send[b, at // nr, row : row + RIM] = part[k * RIM : (k + 1) * RIM]
        projected = total[b, :, 0:128]
        top = projected.astype(BF16)
        rest = (projected - top.astype(F32)).astype(BF16)
        term = (dot(left_test[...], top) + dot(left_test[...], rest)).astype(BF16)
        for k in range(left_test.shape[0] // RIM):
            at = k * RIM
            row = nr + at % nc
            tm_send[b, at // nc, row : row + RIM] = term[k * RIM : (k + 1) * RIM]
        copies = [
            send(tm_send.at[b, peer("tm", d)], tm_recv.at[b, d - 1], tm_sems, "tm", d, b)
            for d in range(1, times)
        ]
        started.extend(copies)
        return copies

    def sum_terms(b, copies):
        summed = tm_send[b, here_t].astype(F32)
        for d in range(1, times):
            copies[d - 1].wait_recv()
            summed += tm_recv[b, d - 1].astype(F32)
        rall[b, here_t] = summed[0:nr].astype(BF16)
        call[b, here_c] = summed[nr : nr + nc].astype(BF16)
        over_c = [
            send(call.at[b, here_c], call.at[b, here_c], call_sems, "chan", d, b)
            for d in range(1, blocks)
        ]
        over_t = [
            send(rall.at[b, here_t], rall.at[b, here_t], r_sems, "tm", d, b)
            for d in range(1, times)
        ]
        started.extend(over_c + over_t)
        return over_c, over_t

    def sum_core(b, copies):
        for copy in copies:
            copy.wait_recv()
        c_sum = call[b, 0].astype(F32)
        for p in range(1, blocks):
            c_sum += call[b, p].astype(F32)
        csend[b, here_t] = c_sum
        over_t = [
            send(csend.at[b, here_t], csend.at[b, here_t], c_sems, "tm", d, b)
            for d in range(1, times)
        ]
        started.extend(over_t)
        return over_t

    def store_range(b, copies):
        for copy in copies:
            copy.wait_recv()
        for c in range(rows // 128):
            for k in range(rank // RIM):
                at = c * rank + k * RIM
                part = rall[b, at // nr, at % nr : at % nr + RIM, :]
                rout[b, k * RIM : (k + 1) * RIM, c * 128 : (c + 1) * 128] = part.astype(F32)

    terms, sums, cores = {}, {}, {}
    for b in range(bands):
        filter_band(b)
        terms[b] = spread_terms(b)
        if b == 0:
            y_sum = y_send[here_c].astype(F32)
            for d in range(1, blocks):
                y_copies[d - 1].wait_recv()
                y_sum += y_recv[d - 1].astype(F32)
            yall[here_c] = y_sum.astype(BF16)
            yall_copies = [
                send(yall.at[here_c], yall.at[here_c], yall_sems, "chan", d) for d in range(1, blocks)
            ]
        if b >= 1:
            sums[b - 1] = sum_terms(b - 1, terms[b - 1])
        if b >= 2:
            cores[b - 2] = sum_core(b - 2, sums[b - 2][0])
    final = bands - 1
    sums[final] = sum_terms(final, terms[final])
    for b in range(max(bands - 2, 0), final):
        cores[b] = sum_core(b, sums[b][0])
    for b in range(final):
        store_range(b, sums[b][1])
    for copy in yall_copies:
        copy.wait_recv()
    for p in range(blocks):
        block = yall[p].astype(F32)[: piece * (span // width)]
        if width < span:
            block = jnp.concatenate(
                [block[k * piece : (k + 1) * piece] for k in range(span // width)], axis=1
            )
        yfull[p * piece : (p + 1) * piece, :] = block
    window = jnp.concatenate(
        [yfull[:, k : k + 2 * WIDE].astype(BF16) for k in range(0, samples, WIDE)], axis=0
    )
    for b in range(bands):
        result = dot(window, toep[b])
        for k in range(samples // WIDE):
            yout[b, :, k * WIDE : (k + 1) * WIDE] = result[k * corank : (k + 1) * corank]

    cores[final] = sum_core(final, sums[final][0])
    store_range(final, sums[final][1])
    for b in range(bands):
        for copy in cores[b]:
            copy.wait_recv()
        for q in range(times):
            cout[b * times * nc + q * nc : b * times * nc + (q + 1) * nc, :] = csend[b, q]
    for copy in started + y_copies + yall_copies:
        copy.wait_send()
    for copy in out_copies:
        copy.wait()


def on_device(recording, band_taps, channel_gain, range_test, corange_test, core_left, core_right):
    rows, samples = recording.shape
    bands, taps = band_taps.shape
    span = samples + 2 * EDGE
    rank, core_rank, corank = range_test.shape[1], core_left.shape[0], corange_test.shape[0]
    times, blocks = lax.axis_size("tm"), lax.axis_size("chan")
    nr, nc = rank * rows // 128 // times, core_rank // times
    piece = corank // blocks
    fold = max(1, RIM // piece)
    if span % (fold * 128):
        fold = 1
    tile = (max(RIM, piece), span // fold)
    vmem = pl.BlockSpec(memory_space=pltpu.VMEM)
    anywhere = pl.BlockSpec(memory_space=pltpu.HBM)

    def sems(count, parts=1):
        return pltpu.SemaphoreType.DMA((2, parts * (count - 1)))

    strain, ranges, corange_sketch, core_sketch = pl.pallas_call(
        fused_kernel,
        in_specs=[anywhere] + [vmem] * 2 + [anywhere] * 4,
        out_specs=[anywhere] + [vmem] * 3,
        out_shape=[
            jax.ShapeDtypeStruct((bands, rows, samples), BF16),
            jax.ShapeDtypeStruct((bands, rank, rows), F32),
            jax.ShapeDtypeStruct((bands, corank, samples), F32),
            jax.ShapeDtypeStruct((bands * core_rank, core_rank), F32),
        ],
        scratch_shapes=[
            pltpu.VMEM((rows + 2 * RIM, span), BF16),
            pltpu.VMEM((bands, 2 * WIDE, WIDE), BF16),
            pltpu.VMEM((samples, 256), BF16),
            pltpu.VMEM((rows, WIDE), F32),
            pltpu.VMEM((bands, rows, 256), F32),
            pltpu.VMEM((bands, rows, samples), BF16),
            pltpu.SemaphoreType.DMA((bands,)),
            pltpu.VMEM((bands, times, nr + nc, 128), BF16),
            pltpu.VMEM((bands, times - 1, nr + nc, 128), BF16),
            pltpu.VMEM((bands, times, nr, 128), BF16),
            pltpu.VMEM((bands, times, nc, 128), F32),
            pltpu.VMEM((bands, blocks, nc, 128), BF16),
            pltpu.VMEM((blocks,) + tile, BF16),
            pltpu.VMEM((blocks - 1,) + tile, BF16),
            pltpu.VMEM((blocks,) + tile, BF16),
            pltpu.VMEM((corank, span), F32),
            sems(times, bands), sems(times, bands), sems(times, bands), sems(blocks, bands),
            sems(blocks), sems(blocks),
            sems(9),
            pltpu.SemaphoreType.DMA,
            pltpu.VMEM((rank, samples), BF16),
            pltpu.VMEM((samples, core_rank), BF16),
            pltpu.VMEM((corank, rows), BF16),
            pltpu.VMEM((core_rank, rows), BF16),
            pltpu.SemaphoreType.DMA((4,)),
        ],
        compiler_params=pltpu.CompilerParams(
            collective_id=0, has_side_effects=True, vmem_limit_bytes=55 * 2**20
        ),
    )(
        recording,
        jnp.pad(band_taps.astype(F32), ((0, 0), (0, 2 * WIDE - taps))),
        channel_gain[None, :],
        range_test.T,
        core_right,
        corange_test,
        core_left,
    )
    range_sketch = jnp.swapaxes(ranges, 1, 2)
    core_sketch = core_sketch.reshape(bands, core_rank, core_rank)
    return strain, range_sketch, corange_sketch, core_sketch


def solution(mesh):
    in_specs = (
        P("chan", "tm"),
        P(),
        P("chan"),
        P("tm", None),
        P(None, "chan"),
        P(None, "chan"),
        P("tm", None),
    )
    out_specs = (P(None, "chan", "tm"), P(None, "chan", None), P(None, None, "tm"), P())
    return jax.shard_map(
        on_device, mesh=mesh, in_specs=in_specs, out_specs=out_specs, check_vma=False
    )
```
